32 devices in a mesh: row: 4 (over x, core), col: 8 (over z, y).
Axes of the slice: x: 2, y: 2, z: 4, core: 2. Of those that a mesh axis runs over, the one named last changes fastest.
Arguments:
- lambda_amps: float32 [256, 32768], P('row', 'col'), may hold values from -6 to 6
- integrals: float32 [32768, 16384], P('col', 'row'), may hold values from -0.046875 to 0.046875
- symmetry_map: int32 [256, 128], P('col', 'row'), may hold values 0 or 1
- base_residual: float32 [256, 16384], P('col', 'row'), may hold values from -6 to 6
Outputs:
- residual: float32 [256, 16384], P('col', 'row')
The draws below stay inside these ranges and needn't reach their ends.
All inputs are finite; a program needn't handle non-finite values. No bound on the sum of `symmetry_map` on one device may be relied on, other than what follows from the above.
Results may differ from the reference program's by a relative error of at most 0.0001.
Values sent between devices are 32-bit elements; how exact they have to be, the bound alone decides.
No kernel may reach another device: no remote copies, remote signals or barrier semaphores. Data moves between devices by JAX's collectives and lax.ppermute only.
A program may use at most 192 MiB of HBM per device.

```python
import jax
import jax.numpy as jnp
from jax import lax

TILE = 128
PAIRS = 256
KCD = 32768
NAB = 16384


def with_ends(entries, key, low, largest):
    shape = entries.shape
    index_at = [jax.random.randint(jax.random.fold_in(key, axis), (), 0, shape[axis]) for axis in range(len(shape))]
    entries = entries.at[tuple(index_at)].set(low)
    longest = shape.index(max(shape))
    index_at[longest] = (index_at[longest] + 1) % shape[longest]
    return entries.at[tuple(index_at)].set(largest)


def raised(drawn, rng, source, target, parts, factor):
    def block_of(dim):
        return (jnp.arange(drawn.shape[dim]) // (drawn.shape[dim] // parts)).reshape((-1,) + (1,) * (drawn.ndim - 1 - dim))

    one_side = jax.random.permutation(rng, parts)[block_of(target)]
    far = (block_of(target) + parts // 2) % parts
    return jnp.where((block_of(source) == one_side) | (block_of(source) == far), factor * drawn, drawn)


def block_scale(stream_key, dims, cuts, least, largest):
    factor_of = 1.0
    for dim, shards_of in cuts:
        steps = jax.random.uniform(jax.random.fold_in(jax.random.fold_in(stream_key, 6), dim), (shards_of,), jnp.float32, least / len(cuts), largest / len(cuts))
        factor_of = factor_of * jnp.repeat(jnp.exp(steps), dims[dim] // shards_of).reshape((-1,) + (1,) * (len(dims) - 1 - dim))
    return factor_of


def bell_draw(key, dims, scale, bound, cuts=(), held_as=jnp.bfloat16):
    array = jax.random.normal(key, dims, jnp.float32) * scale
    if len(cuts) > 0:
        array = block_scale(key, dims, cuts, -0.22, 0.18) * array
    return jnp.clip(array, min=-bound, max=bound).astype(held_as)


def bell_draw_with(own_key, extent, deviation, bound, split, heavy, held_as=jnp.bfloat16):
    drawn = deviation * jax.random.normal(own_key, extent, jnp.float32)
    if split:
        drawn = drawn * block_scale(own_key, extent, split, -0.22, 0.18)
    return jnp.clip(raised(drawn, jax.random.fold_in(own_key, 3), *heavy), -bound, bound).astype(held_as)


def setup_inputs(seed: int = 0) -> dict:
    key_of = jax.random.split(jax.random.key(seed), 5)
    return {
        "lambda_amps": bell_draw_with(key_of[0], (PAIRS, KCD), 1.0, 6.0, ((0, 4), (1, 8)), (1, 0, 8, 2.0), jnp.float32),
        "integrals": bell_draw(key_of[1], (KCD, NAB), (KCD // 2) ** -0.5, 0.046875, ((0, 8), (1, 4)), jnp.float32),
        "symmetry_map": with_ends((jax.random.randint(key_of[2], (KCD // TILE, NAB // TILE), 0, 2) < 1).astype(jnp.int32), jax.random.fold_in(key_of[2], 1), 0, 1),
        "base_residual": bell_draw(key_of[3], (PAIRS, NAB), 1.0, 6.0, ((0, 8), (1, 4)), jnp.float32),
    }


def reference(lambda_amps, integrals, symmetry_map, base_residual):
    blocks = KCD // TILE
    lam_blocks = lambda_amps.reshape(PAIRS, blocks, TILE).transpose(1, 0, 2)
    int_blocks = integrals.reshape(blocks, TILE, NAB)
    flags = symmetry_map.astype(jnp.float32)

    def step(total, items):
        lam_piece, int_piece, flag_row = items
        wide = jnp.repeat(flag_row, TILE)
        masked = int_piece * wide[None, :]
        return total + jnp.dot(lam_piece, masked, preferred_element_type=jnp.float32, precision=lax.Precision.HIGHEST), None

    ladder, _ = lax.scan(step, jnp.zeros((PAIRS, NAB), jnp.float32), (lam_blocks, int_blocks, flags))
    return base_residual + ladder
```

```python
import functools

import jax
import jax.numpy as jnp
from jax import lax
from jax.experimental import pallas as pl
from jax.experimental.pallas import tpu as pltpu
from jax.sharding import PartitionSpec as P

TILE = 128
WIDE = 2 * TILE
F32, BF16 = jnp.float32, jnp.bfloat16
GROUP = 4
DEPTH = 3
VMEM = pl.BlockSpec(memory_space=pltpu.VMEM)
SMEM = pl.BlockSpec(memory_space=pltpu.SMEM)


def block_lists(flags):
    kb, nb = flags.shape
    on = (flags != 0).reshape(kb, nb // 2, 2).astype(jnp.int32)
    either = on[..., 0] | on[..., 1]
    place = jnp.arange(kb, dtype=jnp.int32)
    code = place[:, None] * 4 + on[..., 0] + 2 * on[..., 1]
    lower = (place[:, None] > place[None, :]).astype(jnp.int32)
    rank = jnp.sum(lower[:, :, None] * either[None], axis=1)
    hit = (rank[None] == place[:, None, None]) & (either[None] != 0)
    listed = jnp.sum(jnp.where(hit, code[None], 0), axis=1)
    count = jnp.sum(either, axis=0)
    listed = jnp.where(place[:, None] < count[None], listed, kb * 4)
    return listed.T.reshape(-1), (count + GROUP - 1) // GROUP


def split_rows(o_ref, first, x):
    rows, half = x.shape[0], o_ref.shape[1] // 2
    for p in range(x.shape[1] // TILE):
        part = x[:, p * TILE : (p + 1) * TILE]
        high = part.astype(BF16)
        o_ref[p, first : first + rows] = high
        o_ref[p, half + first : half + first + rows] = (part - high.astype(F32)).astype(BF16)


def order_kernel(at_ref, own_ref, mate_ref, o_ref):
    y, z1, core = at_ref[0], at_ref[1], at_ref[2]
    o_ref[o_ref.shape[0] - 1] = jnp.zeros(o_ref.shape[1:], BF16)
    part = own_ref.shape[0] // 2
    for j in range(4):
        row = y if j >= 2 else 1 - y
        side = z1 if j % 2 else 1 - z1
        rows = pl.ds(pl.multiple_of(row * part, part), part)

        @pl.when(side == core)
        def _():
            split_rows(o_ref, j * part, own_ref[rows])

        @pl.when(side != core)
        def _():
            split_rows(o_ref, j * part, mate_ref[rows])


def ordered(at, own, mate):
    m, k = own.shape
    return pl.pallas_call(
        order_kernel,
        out_shape=jax.ShapeDtypeStruct((k // TILE + 1, 4 * m, TILE), BF16),
        in_specs=[SMEM, VMEM, VMEM],
        out_specs=VMEM,
        compiler_params=pltpu.CompilerParams(vmem_limit_bytes=24 * 2**20),
        cost_estimate=pl.CostEstimate(flops=8 * m * k, bytes_accessed=16 * m * k, transcendentals=0),
    )(at, own, mate)


def plain_kernel(l_ref, o_ref):
    o_ref[o_ref.shape[0] - 1] = jnp.zeros(o_ref.shape[1:], BF16)
    split_rows(o_ref, 0, l_ref[...])


def plain(lam):
    m, k = lam.shape
    return pl.pallas_call(
        plain_kernel,
        out_shape=jax.ShapeDtypeStruct((k // TILE + 1, 2 * m, TILE), BF16),
        in_specs=[VMEM],
        out_specs=VMEM,
        compiler_params=pltpu.CompilerParams(vmem_limit_bytes=24 * 2**20),
    )(lam)


def ladder_kernel(first, pairs, kb, list_ref, count_ref, l_ref, g_ref, send_ref, keep_ref, buf, sem):
    m = l_ref.shape[1] // 2

    def start(q, slot):
        def some(c, _):
            for u in range(GROUP):
                p = lax.shift_right_logical(list_ref[q * kb + c * GROUP + u], 2)
                p = jnp.where(p == kb, 0, p)
                pltpu.make_async_copy(
                    g_ref.at[pl.ds(pl.multiple_of(p * TILE, TILE), TILE), pl.ds(pl.multiple_of(q * WIDE, WIDE), WIDE)],
                    buf.at[slot, pl.ds(pl.multiple_of((c * GROUP + u) * TILE, TILE), TILE)],
                    sem.at[slot],
                ).start()
            return 0

        lax.fori_loop(0, count_ref[q], some, 0)

    def wait(q, slot):
        def some(c, _):
            rows = pl.ds(0, GROUP * TILE)
            pltpu.make_async_copy(g_ref.at[rows, pl.ds(0, WIDE)], buf.at[slot, rows], sem.at[slot]).wait()
            return 0

        lax.fori_loop(0, count_ref[q], some, 0)

    for d in range(min(DEPTH - 1, pairs)):
        start(first + d, d)

    def step(i, _):
        q, slot, ahead = first + i, lax.rem(i, DEPTH), i + DEPTH - 1

        @pl.when(ahead < pairs)
        def _():
            start(first + ahead, lax.rem(ahead, DEPTH))

        wait(q, slot)
        columns = pl.ds(pl.multiple_of(i * WIDE, WIDE), WIDE)
        count = count_ref[q]
        for c in range(kb // GROUP + 1):

            @pl.when(count == c)
            def _():
                both, low = jnp.zeros((2 * m, WIDE), F32), jnp.zeros((m, WIDE), F32)
                for k in range(0, c * GROUP, 2):
                    lefts, rights = [], []
                    for u in (k, k + 1):
                        code = list_ref[q * kb + u]
                        lefts.append(l_ref[lax.shift_right_logical(code, 2)])
                        rows = pl.ds(u * TILE, TILE)
                        rights.append(
                            jnp.concatenate(
                                [
                                    buf[slot, rows, 0:TILE] * (code & 1).astype(F32),
                                    buf[slot, rows, TILE:WIDE] * (lax.shift_right_logical(code, 1) & 1).astype(F32),
                                ],
                                axis=1,
                            )
                        )
                    left, right = jnp.concatenate(lefts, axis=1), jnp.concatenate(rights, axis=0)
                    high = right.astype(BF16)
                    rest = (right - high.astype(F32)).astype(BF16)
                    both = both + jnp.dot(left, high, preferred_element_type=F32)
                    low = low + jnp.dot(left[:m], rest, preferred_element_type=F32)
                total = both[:m] + (both[m:] + low)
                send_ref[:, columns] = total[: m // 2]
                keep_ref[:, columns] = total[m // 2 :]

        return 0

    lax.fori_loop(0, pairs, step, 0)


def ladder(lists, left, integrals, first, pairs):
    kb, m = left.shape[0] - 1, left.shape[1] // 2
    out = jax.ShapeDtypeStruct((m // 2, pairs * WIDE), F32)
    return pl.pallas_call(
        functools.partial(ladder_kernel, first, pairs, kb),
        out_shape=[out, out],
        in_specs=[SMEM, SMEM, VMEM, pl.BlockSpec(memory_space=pl.ANY)],
        out_specs=[VMEM, VMEM],
        scratch_shapes=[pltpu.VMEM((DEPTH, kb * TILE, WIDE), F32), pltpu.SemaphoreType.DMA((DEPTH,))],
        compiler_params=pltpu.CompilerParams(vmem_limit_bytes=32 * 2**20),
        cost_estimate=pl.CostEstimate(
            flops=24 * m * kb * TILE * pairs * WIDE, bytes_accessed=4 * kb * TILE * pairs * WIDE, transcendentals=0
        ),
    )(*lists, left, integrals)


def body_any(lambda_amps, integrals, symmetry_map, base_residual):
    lists = block_lists(symmetry_map)
    gathered = lax.all_gather(lambda_amps, "row", axis=0, tiled=True)
    pairs = integrals.shape[1] // WIDE
    sums = []
    for first in range(0, gathered.shape[0], TILE):
        sums += ladder(lists, plain(gathered[first : first + TILE]), integrals, 0, pairs)
    return base_residual + lax.psum_scatter(jnp.concatenate(sums), "col", scatter_dimension=0, tiled=True)


NEAR = (7, 7, 2)
FAR = (8, 5, 3)


def body_cube(rows, cols, lambda_amps, integrals, symmetry_map, base_residual):
    row, col = lax.axis_index("row"), lax.axis_index("col")
    x, core = row // 2, row % 2
    y, z1, z2 = col % 2, col // 2 % 2, col // 4
    at = jnp.stack([y, z1, core]).astype(jnp.int32)

    def swap(array, axis, step):
        n = rows if axis == "row" else cols
        return lax.ppermute(array, axis, [(i, i ^ step) for i in range(n)])

    def across(array, near):
        hops = []
        for r in range(rows):
            for c in range(cols):
                if (r // 2 != c // 4) == near:
                    hops.append((r * cols + c, r * cols + (c ^ 4)))
        return lax.ppermute(array, ("row", "col"), hops)

    def after(array, *earlier):
        return lax.optimization_barrier((array, *earlier))[0]

    far = swap(lambda_amps, "row", 2)
    mate = swap(lambda_amps, "row", 1)
    lists = block_lists(symmetry_map)
    part = lambda_amps.shape[0] // 2
    cuts = [(True, pairs) for pairs in NEAR] + [(False, pairs) for pairs in FAR]
    left = ordered(at, lambda_amps, mate)
    y_sent, z1_sent, z2_sent, done, fresh = [], [], [], [], []
    first = 0

    def finish_y(i, *earlier):
        keep, there = y_sent[i]
        total = keep + after(there, *earlier)
        z1_sent.append((total[part:], swap(total[:part], "col", 2)))
        fresh.append(total)

    def finish_z1(i, *earlier):
        keep, there = z1_sent[i]
        total = keep + after(there, *earlier)
        z2_sent.append((total, across(total, cuts[i][0])))
        fresh.append(total)

    def finish_z2(i, *earlier):
        keep, there = z2_sent[i]
        done.append(keep + after(there, *earlier))
        fresh.append(done[-1])

    for step, (near, pairs) in enumerate(cuts):
        if step == len(NEAR) - 1:
            far = after(far, fresh[-1])
            far_mate = swap(far, "row", 1)
        if step == len(NEAR):
            first = 0
            left = ordered(at, far, after(far_mate, fresh[-1]))
        if step > 0:
            left = after(left, *fresh)
            fresh.clear()
        send, keep = ladder(lists, left, integrals, first, pairs)
        first += pairs
        fresh.append(keep)
        y_sent.append((keep, swap(send, "col", 1)))
        if step >= 3:
            finish_z2(step - 3, keep)
        if step >= 2:
            finish_z1(step - 2, keep)
        if step >= 1:
            finish_y(step - 1, keep)
    last = len(cuts) - 1
    finish_z1(last - 1)
    finish_y(last)
    finish_z1(last)
    for i in range(last - 2, last + 1):
        finish_z2(i)
    near_sum = jnp.concatenate(done[: len(NEAR)], axis=1)
    far_sum = jnp.concatenate(done[len(NEAR) :], axis=1)
    return base_residual + jnp.where(z2 == x, near_sum, far_sum)


def solution(mesh):
    placed = (P("row", "col"), P("col", "row"), P("col", "row"), P("col", "row"))
    rows, cols = mesh.shape["row"], mesh.shape["col"]
    body = functools.partial(body_cube, rows, cols) if (rows, cols) == (4, 8) else body_any
    return jax.shard_map(body, mesh=mesh, in_specs=placed, out_specs=P("col", "row"), check_vma=False)
```

```python
import functools

import jax
import jax.numpy as jnp
from jax import lax
from jax.experimental import pallas as pl
from jax.experimental.pallas import tpu as pltpu
from jax.sharding import PartitionSpec as P

TILE = 128
WIDE = 2 * TILE
F32, BF16 = jnp.float32, jnp.bfloat16
GROUP = 4
DEPTH = 3
VMEM = pl.BlockSpec(memory_space=pltpu.VMEM)
SMEM = pl.BlockSpec(memory_space=pltpu.SMEM)


def block_lists(flags):
    kb, nb = flags.shape
    on = (flags != 0).reshape(kb, nb // 2, 2).astype(jnp.int32)
    left, right = on[..., 0], on[..., 1]
    at = jnp.arange(kb, dtype=jnp.int32)
    key = (3 - 2 * left - right + 3 * (1 - jnp.maximum(left, right))) * kb + at[:, None]
    place = jnp.sum((key[None] < key[:, None]).astype(jnp.int32), axis=1)
    code = jnp.where(left + right > 0, at[:, None] * 4 + left + 2 * right, kb * 4)
    used = jnp.sum(jnp.where(place[None] == at[:, None, None], code[None], 0), axis=1)
    kinds = jnp.stack([left * right, left * (1 - right), right * (1 - left)])
    return used.T.reshape(-1), jnp.sum(kinds, axis=1).reshape(-1)


def split_rows(o_ref, first, x):
    rows, half = x.shape[0], o_ref.shape[1] // 2
    for p in range(x.shape[1] // TILE):
        part = x[:, p * TILE : (p + 1) * TILE]
        high = part.astype(BF16)
        o_ref[p, first : first + rows] = high
        o_ref[p, half + first : half + first + rows] = (part - high.astype(F32)).astype(BF16)


def counts_of(q, count_ref):
    pairs = count_ref.shape[0] // 3
    return count_ref[q], count_ref[pairs + q], count_ref[2 * pairs + q]


def blocks_in(q, kb, list_ref, count_ref, g_ref, buf, slot, sem):
    def kind(begin, count, side, width):
        def one(j):
            p = lax.shift_right_logical(list_ref[q * kb + j], 2)
            pltpu.make_async_copy(
                g_ref.at[
                    pl.ds(pl.multiple_of(p * TILE, TILE), TILE),
                    pl.ds(pl.multiple_of(q * WIDE + side * TILE, TILE), width),
                ],
                buf.at[slot, pl.ds(pl.multiple_of(j * TILE, TILE), TILE), pl.ds(side * TILE, width)],
                sem,
            ).start()

        fours = lax.shift_right_logical(count, 2)

        def some(c, _):
            for u in range(4):
                one(begin + c * 4 + u)
            return 0

        def rest(c, _):
            one(begin + fours * 4 + c)
            return 0

        lax.fori_loop(0, fours, some, 0)
        lax.fori_loop(0, count & 3, rest, 0)

    both, left, right = counts_of(q, count_ref)
    kind(0, both, 0, WIDE)
    kind(both, left, 0, TILE)
    kind(both + left, right, 1, TILE)


def blocks_wait(q, count_ref, g_ref, buf, slot, sem):
    both, left, right = counts_of(q, count_ref)
    count = 2 * both + left + right

    def some(blocks):
        rows = pl.ds(0, blocks * TILE)

        def body(c, _):
            pltpu.make_async_copy(g_ref.at[rows, pl.ds(0, TILE)], buf.at[slot, rows, pl.ds(0, TILE)], sem).wait()
            return 0

        return body

    lax.fori_loop(0, lax.shift_right_logical(count, 3), some(8), 0)
    lax.fori_loop(0, count & 7, some(1), 0)


def order_kernel(bring, at_ref, list_ref, count_ref, own_ref, mate_ref, g_ref, o_ref, *rest):
    y, z1, core = at_ref[0], at_ref[1], at_ref[2]
    if bring:
        buf, own, own_sem, sem = rest
        kb = o_ref.shape[0] - 1
        copy = pltpu.make_async_copy(own_ref, own, own_sem)
        copy.start()
        blocks_in(0, kb, list_ref, count_ref, g_ref, buf, 0, sem)
    else:
        own = own_ref
    o_ref[o_ref.shape[0] - 1] = jnp.zeros(o_ref.shape[1:], BF16)
    part = own_ref.shape[0] // 2

    def put(source, mine):
        for j in range(4):
            row = y if j >= 2 else 1 - y
            side = z1 if j % 2 else 1 - z1
            rows = pl.ds(pl.multiple_of(row * part, part), part)

            @pl.when((side == core) == mine)
            def _():
                split_rows(o_ref, j * part, source[rows])

    put(mate_ref, False)
    if bring:
        copy.wait()
    put(own, True)
    if bring:
        blocks_wait(0, count_ref, g_ref, buf, 0, sem)


def ordered(at, lists, own, mate, integrals, bring):
    m, k = own.shape
    shape = jax.ShapeDtypeStruct((k // TILE + 1, 4 * m, TILE), BF16)
    ring = jax.ShapeDtypeStruct((DEPTH, k, WIDE), F32)
    whole = pl.BlockSpec(memory_space=pl.ANY)
    return pl.pallas_call(
        functools.partial(order_kernel, bring),
        out_shape=[shape, ring] if bring else [shape],
        in_specs=[SMEM, SMEM, SMEM, whole if bring else VMEM, VMEM, whole],
        out_specs=[VMEM, VMEM] if bring else [VMEM],
        scratch_shapes=[pltpu.VMEM((m, k), F32), pltpu.SemaphoreType.DMA, pltpu.SemaphoreType.DMA] if bring else [],
        compiler_params=pltpu.CompilerParams(vmem_limit_bytes=12 * 2**20),
        cost_estimate=pl.CostEstimate(flops=8 * m * k, bytes_accessed=16 * m * k, transcendentals=0),
    )(at, *lists, own, mate, integrals)


def plain_kernel(l_ref, o_ref):
    o_ref[o_ref.shape[0] - 1] = jnp.zeros(o_ref.shape[1:], BF16)
    split_rows(o_ref, 0, l_ref[...])


def plain(lam):
    m, k = lam.shape
    return pl.pallas_call(
        plain_kernel,
        out_shape=jax.ShapeDtypeStruct((k // TILE + 1, 2 * m, TILE), BF16),
        in_specs=[VMEM],
        out_specs=VMEM,
        compiler_params=pltpu.CompilerParams(vmem_limit_bytes=12 * 2**20),
    )(lam)


def ladder_kernel(first, pairs, after, begin, kb, list_ref, count_ref, l_ref, g_ref, *rest):
    send_ref, keep_ref, buf, sem = rest[-4:]
    m = l_ref.shape[1] // 2
    slot_of = lambda i: lax.rem(i + (begin or 0), DEPTH)

    def start(q, i):
        blocks_in(q, kb, list_ref, count_ref, g_ref, buf, slot_of(i), sem.at[slot_of(i)])

    def wait(q, i):
        blocks_wait(q, count_ref, g_ref, buf, slot_of(i), sem.at[slot_of(i)])

    for d in range(0 if begin is None else 1, min(DEPTH - 1, pairs)):
        start(first + d, d)
    if after is not None and pairs < DEPTH - 1:
        start(after, pairs)

    def step(i, _):
        q, slot, ahead = first + i, slot_of(i), i + DEPTH - 1

        @pl.when(ahead < pairs)
        def _():
            start(first + ahead, ahead)

        if after is not None and pairs >= DEPTH - 1:

            @pl.when(ahead == pairs)
            def _():
                start(after, ahead)

        if begin is None:
            wait(q, i)
        else:

            @pl.when(i > 0)
            def _():
                wait(q, i)

        columns = pl.ds(pl.multiple_of(i * WIDE, WIDE), WIDE)
        groups = (sum(counts_of(q, count_ref)) + GROUP - 1) // GROUP
        for c in range(kb // GROUP + 1):

            @pl.when(groups == c)
            def _():
                both, low = jnp.zeros((2 * m, WIDE), F32), jnp.zeros((m, WIDE), F32)
                for k in range(0, c * GROUP, 2):
                    lefts, rights = [], []
                    for u in (k, k + 1):
                        code = list_ref[q * kb + u]
                        lefts.append(l_ref[lax.shift_right_logical(code, 2)])
                        rows = pl.ds(u * TILE, TILE)
                        sides = [
                            jnp.where((code & (side + 1)) != 0, buf[slot, rows, side * TILE : (side + 1) * TILE], 0.0)
                            for side in range(2)
                        ]
                        rights.append(jnp.concatenate(sides, axis=1))
                    left, right = jnp.concatenate(lefts, axis=1), jnp.concatenate(rights, axis=0)
                    high = right.astype(BF16)
                    rest = (right - high.astype(F32)).astype(BF16)
                    both = both + jnp.dot(left, high, preferred_element_type=F32)
                    low = low + jnp.dot(left[:m], rest, preferred_element_type=F32)
                total = both[:m] + (both[m:] + low)
                send_ref[:, columns] = total[: m // 2]
                keep_ref[:, columns] = total[m // 2 :]

        return 0

    lax.fori_loop(0, pairs, step, 0)
    if after is not None:
        wait(after, pairs)


def ladder(lists, left, integrals, first, pairs, ring=None, begin=None, after=None):
    kb, m = left.shape[0] - 1, left.shape[1] // 2
    out = jax.ShapeDtypeStruct((m // 2, pairs * WIDE), F32)
    buffer = jax.ShapeDtypeStruct((DEPTH, kb * TILE, WIDE), F32)
    chained = ring is not None
    return pl.pallas_call(
        functools.partial(ladder_kernel, first, pairs, after, begin, kb),
        out_shape=[out, out, buffer] if chained else [out, out],
        in_specs=[SMEM, SMEM, VMEM, pl.BlockSpec(memory_space=pl.ANY)] + [VMEM] * chained,
        out_specs=[VMEM, VMEM] + [VMEM] * chained,
        input_output_aliases={4: 2} if chained else {},
        scratch_shapes=([] if chained else [pltpu.VMEM(buffer.shape, F32)]) + [pltpu.SemaphoreType.DMA((DEPTH,))],
        compiler_params=pltpu.CompilerParams(vmem_limit_bytes=16 * 2**20),
        cost_estimate=pl.CostEstimate(
            flops=24 * m * kb * TILE * pairs * WIDE, bytes_accessed=4 * kb * TILE * pairs * WIDE, transcendentals=0
        ),
    )(*lists, left, integrals, *([ring] if chained else []))


def body_any(lambda_amps, integrals, symmetry_map, base_residual):
    lists = block_lists(symmetry_map)
    gathered = lax.all_gather(lambda_amps, "row", axis=0, tiled=True)
    pairs = integrals.shape[1] // WIDE
    sums = []
    for first in range(0, gathered.shape[0], TILE):
        sums += ladder(lists, plain(gathered[first : first + TILE]), integrals, 0, pairs)
    return base_residual + lax.psum_scatter(jnp.concatenate(sums), "col", scatter_dimension=0, tiled=True)


CHUNKS = (
    (True, 0, 5),
    (True, 5, 6),
    (True, 11, 5),
    (False, 0, 5),
    (False, 5, 5),
    (False, 10, 4),
    (False, 14, 2),
)
FAR_SWAP = 2
ACTIONS = (
    (),
    (("end y", (0,)),),
    (("end y", (1,)), ("z1", (0, 1))),
    (("end y", (2,)), ("z1", (2,)), ("end z1", (1,)), ("z2", (1,))),
    (("end y", (3,)), ("z1", (3,)), ("end z1", (2,)), ("z2", (2,))),
    (("end z1", (3,)), ("z2", (3,)), ("end y", (4,)), ("z1", (4,)), ("end z2", (1,))),
    (
        ("end z1", (4,)),
        ("z2", (4,)),
        ("end y", (5,)),
        ("z1", (5,)),
        ("end z2", (2, 3)),
        ("end y", (6,)),
        ("z1", (6,)),
        ("end z1", (5,)),
        ("z2", (5,)),
        ("end z1", (6,)),
        ("z2", (6,)),
        ("end z2", (4, 5, 6)),
    ),
)
NEAR_PARTS = (1, 2)
FAR_PARTS = (3, 4, 5, 6)


def body_cube(rows, cols, lambda_amps, integrals, symmetry_map, base_residual):
    row, col = lax.axis_index("row"), lax.axis_index("col")
    x, core = row // 2, row % 2
    y, z1, z2 = col % 2, col // 2 % 2, col // 4
    at = jnp.stack([y, z1, core]).astype(jnp.int32)

    def swap(array, axis, step):
        n = rows if axis == "row" else cols
        return lax.ppermute(array, axis, [(i, i ^ step) for i in range(n)])

    def across(array, near):
        hops = []
        for r in range(rows):
            for c in range(cols):
                if (r // 2 != c // 4) == near:
                    hops.append((r * cols + c, r * cols + (c ^ 4)))
        return lax.ppermute(array, ("row", "col"), hops)

    def after(array, *earlier):
        return lax.optimization_barrier((array, *earlier))[0]

    far = swap(lambda_amps, "row", 2)
    mate = swap(lambda_amps, "row", 1)
    lists = block_lists(symmetry_map)
    part = lambda_amps.shape[0] // 2
    left, ring = ordered(at, lists, lambda_amps, mate, integrals, True)
    lefts = {True: left}
    kept, fresh = [], []
    sent, landed = {}, {}

    def land(hop, key, last):
        keep, there = sent.pop((hop, key))
        landed[hop, key] = keep + after(there, fresh[-1] if last else kept[-1])
        fresh.append(landed[hop, key])

    def join(hop, keys):
        return jnp.concatenate([landed[hop, key] for key in keys], axis=1) if len(keys) > 1 else landed[hop, keys[0]]

    begin = 0
    for step, (near, first, pairs) in enumerate(CHUNKS):
        if step == FAR_SWAP:
            far = after(far, kept[-1])
            far_mate = swap(far, "row", 1)
        if near not in lefts:
            lefts[near] = ordered(at, lists, far, after(far_mate, kept[-1]), integrals, False)[0]
        left = after(lefts[near], *fresh) if fresh else lefts[near]
        fresh.clear()
        following = CHUNKS[step + 1][1] if step + 1 < len(CHUNKS) else None
        send, keep, ring = ladder(lists, left, integrals, first, pairs, ring, begin, following)
        begin = (begin + pairs) % DEPTH
        kept.append(keep)
        fresh.append(keep)
        sent["y", step] = keep, swap(send, "col", 1)
        for hop, keys in ACTIONS[step]:
            last = step + 1 == len(CHUNKS)
            if hop == "z1":
                total = join("y", keys)
                sent["z1", keys[-1]] = total[part:], swap(total[:part], "col", 2)
            elif hop == "z2":
                total = join("z1", keys)
                sent["z2", keys[-1]] = total, across(total, CHUNKS[keys[-1]][0])
            else:
                for key in keys:
                    land(hop[4:], key, last)
    return base_residual + jnp.where(z2 == x, join("z2", NEAR_PARTS), join("z2", FAR_PARTS))


def solution(mesh):
    placed = (P("row", "col"), P("col", "row"), P("col", "row"), P("col", "row"))
    rows, cols = mesh.shape["row"], mesh.shape["col"]
    body = functools.partial(body_cube, rows, cols) if (rows, cols) == (4, 8) else body_any
    return jax.shard_map(body, mesh=mesh, in_specs=placed, out_specs=P("col", "row"), check_vma=False)
```
